256 devices in a mesh: dp: 16 (over y_hi, x, core), seq: 16 (over y_lo, z).
Axes of the slice: x: 4, y: 4 (y_hi: 2, y_lo: 2; y = y_hi * 2 + y_lo), z: 8, core: 2. Of those that a mesh axis runs over, the one named last changes fastest.
Arguments:
- queries: bfloat16 [16, 2048, 2048], P('dp', None, 'seq'), may hold values from -12 to 12
- key_states: bfloat16 [16, 2048, 2048], P('dp', None, 'seq'), may hold values from -12 to 12
- value_states: bfloat16 [16, 2048, 2048], P('dp', None, 'seq'), may hold values from -6 to 6
- grad_payload: bfloat16 [16, 2048, 2048], P('dp', 'seq'), may hold values from -6 to 6
- grad_scale: bfloat16 [16, 2048, 32], P('dp', 'seq'), may hold values from 0.25 to 4
- inputs: bfloat16 [16, 2048, 3072], P('dp', 'seq'), may hold values from -6 to 6
- lengths: int32 [16], P('dp'), may hold values from 1024 to 2048, as said below
Outputs:
- grad_queries: bfloat16 [16, 2048, 2048], P('dp', 'seq')
- grad_keys: bfloat16 [16, 2048, 2048], P('dp', 'seq')
- grad_values: bfloat16 [16, 2048, 2048], P('dp', 'seq')
- weight_grad: float32 [3, 3072, 2048], P(None, 'dp', 'seq')
The draws below stay inside these ranges and needn't reach their ends.
Inputs may be any that keep to these rules, and one draw needn't show every extreme that they name: `lengths`: padding follows a clip's valid tokens; some clip fills all 2048 tokens.
All inputs are finite; a program needn't handle non-finite values.
Results may differ from the reference program's by a relative error of at most 0.0061.
Values may be sent and summed in bfloat16 or wider, within the bound.
A program may use at most 128 MiB of HBM per device.

```python
import math
import jax
import jax.numpy as jnp
from jax import lax

D = 3072
HEAD_DIM = 64
HEADS = 32
SEQ_LEN = 2048
BATCH = 16


def drawn_parts(key):
    key_place = jax.random.fold_in(key, 1)
    stride = SEQ_LEN // 6
    places = jax.random.randint(key_place, (BATCH, 1, HEADS, 3), 0, stride) + jnp.arange(3, dtype=jnp.int32) * stride
    return places.astype(jnp.int32)


def rough_states(key, spread):
    base_key, scale_key = jax.random.split(key)
    base = jax.random.normal(base_key, (BATCH, SEQ_LEN, HEADS, HEAD_DIM), jnp.float32)
    factor = jnp.exp(jax.random.uniform(scale_key, (BATCH, SEQ_LEN, HEADS, 1), jnp.float32, -spread, spread))
    return base * factor


def place_rows(base, places, slot, strength):
    positions = jnp.arange(SEQ_LEN, dtype=jnp.int32).reshape(1, SEQ_LEN, 1)
    hit = (positions == places[..., slot]).astype(jnp.float32)[..., None] * strength
    return base * (1.0 - hit)


def draw_queries(key, part):
    places = drawn_parts(key)
    key = jax.random.fold_in(key, 11)
    spread = 0.0
    strength = 0.0
    states = rough_states(key, spread)
    states = place_rows(states, places, 0, strength)
    return jnp.clip(states, -12.0, 12.0).reshape(BATCH, SEQ_LEN, HEADS * HEAD_DIM).astype(jnp.bfloat16)


def draw_key_states(key, part):
    places = drawn_parts(key)
    key = jax.random.fold_in(key, 23)
    spread = 0.0
    strength = 0.0
    states = rough_states(key, spread)
    states = place_rows(states, places, 1, strength)
    states = place_rows(states, places, 2, strength)
    return jnp.clip(states, -12.0, 12.0).reshape(BATCH, SEQ_LEN, HEADS * HEAD_DIM).astype(jnp.bfloat16)


def draw_lengths(key, part):
    key = jax.random.fold_in(key, 37)
    first_key, second_key = jax.random.split(key)
    drawn = jax.random.randint(first_key, (BATCH,), SEQ_LEN // 2, SEQ_LEN + 1)
    full = jax.random.randint(second_key, (), 0, BATCH)
    return jnp.where(jnp.arange(BATCH) == full, SEQ_LEN, drawn).astype(jnp.int32)


def spiked(values, rng, source, target, blocks, factor):
    def block_of(axis_at):
        return (jnp.arange(values.shape[axis_at]) // (values.shape[axis_at] // blocks)).reshape((-1,) + (1,) * (values.ndim - 1 - axis_at))

    one_side = jax.random.permutation(rng, blocks)[block_of(target)]
    far = (block_of(target) + blocks // 2) % blocks
    return jnp.where((block_of(source) == one_side) | (block_of(source) == far), factor * values, values)


def block_levels(stream_key, dims, cuts, low, high):
    loudness = 1.0
    for axis_at, blocks in cuts:
        heights = jax.random.uniform(jax.random.fold_in(jax.random.fold_in(stream_key, 6), axis_at), (blocks,), jnp.float32, low / len(cuts), high / len(cuts))
        loudness = loudness * jnp.repeat(jnp.exp(heights), dims[axis_at] // blocks).reshape((-1,) + (1,) * (len(dims) - 1 - axis_at))
    return loudness


def gaussian(stream_key, dims, scale, reach, cuts=(), held_as=jnp.bfloat16):
    factor_of = block_levels(stream_key, dims, cuts, -0.22, 0.18) if cuts else 1.0
    result = jax.random.normal(stream_key, dims, jnp.float32) * scale * factor_of
    return jnp.minimum(jnp.maximum(result, -reach), reach).astype(held_as)


def noise_with(key, extent, scale, most, pieces, heavy, kind=jnp.bfloat16):
    values = scale * jax.random.normal(key, extent, jnp.float32)
    if pieces:
        values = values * block_levels(key, extent, pieces, -0.22, 0.18)
    return jnp.clip(spiked(values, jax.random.fold_in(key, 3), *heavy), -most, most).astype(kind)


def setup_inputs(seed: int = 0) -> dict:
    streams_of = jax.random.split(jax.random.key(seed), 8)
    queries = draw_queries(jax.random.fold_in(streams_of[7], 71), 0)
    key_states = draw_key_states(jax.random.fold_in(streams_of[7], 71), 0)
    value_states = gaussian(streams_of[2], (BATCH, SEQ_LEN, HEADS * HEAD_DIM), 1.0, 6.0, ((0, 16), (2, 16)))
    grad_payload = gaussian(streams_of[3], (BATCH, SEQ_LEN, HEADS * HEAD_DIM), 1.0, 6.0, ((0, 16), (1, 16)))
    grad_scale = jnp.clip(jnp.exp(math.log(4.0) - 2.7725887 * jax.random.uniform(streams_of[4], (BATCH, SEQ_LEN, HEADS), jnp.float32) ** block_levels(streams_of[4], (BATCH, SEQ_LEN, HEADS), ((0, 16), (1, 16)), -0.2, 0.2)), 0.25, 4.0).astype(jnp.bfloat16)
    inputs = noise_with(streams_of[5], (BATCH, SEQ_LEN, D), 1.0, 6.0, ((0, 16), (1, 16)), (0, 2, 16, 2.0))
    lengths = draw_lengths(jax.random.fold_in(streams_of[7], 71), 0)
    return dict(queries=queries, key_states=key_states, value_states=value_states, grad_payload=grad_payload, grad_scale=grad_scale, inputs=inputs, lengths=lengths)


def head_backward(query, key_part, value_part, upstream, usable):
    factor = HEAD_DIM ** -0.5
    scores = jnp.dot(query, key_part.T, preferred_element_type=jnp.float32) * factor
    scores = jnp.where(usable[None, :], scores, -1e30)
    highest = jnp.max(scores, axis=1, keepdims=True)
    weights = jnp.exp(scores - highest)
    attention = weights / jnp.sum(weights, axis=1, keepdims=True)
    attention_low = attention.astype(jnp.bfloat16)
    grad_attention = jnp.dot(upstream, value_part.T, preferred_element_type=jnp.float32)
    balance = jnp.sum(attention * grad_attention, axis=1, keepdims=True)
    grad_scores = (attention * (grad_attention - balance) * factor).astype(jnp.bfloat16)
    grad_query = jnp.dot(grad_scores, key_part, preferred_element_type=jnp.float32).astype(jnp.bfloat16)
    grad_key = jnp.dot(grad_scores.T, query, preferred_element_type=jnp.float32).astype(jnp.bfloat16)
    grad_value = jnp.dot(attention_low.T, upstream, preferred_element_type=jnp.float32).astype(jnp.bfloat16)
    return grad_query, grad_key, grad_value


def split_heads(array):
    return array.reshape(SEQ_LEN, HEADS, HEAD_DIM).transpose(1, 0, 2)


def join_heads(array):
    return array.transpose(1, 0, 2).reshape(SEQ_LEN, HEADS * HEAD_DIM)


def clip_backward(items):
    query, key_part, value_part, upstream, length = items
    usable = jnp.arange(SEQ_LEN) < length

    def one_head(parts):
        return head_backward(parts[0], parts[1], parts[2], parts[3], usable)

    grad_query, grad_key, grad_value = lax.map(one_head, (split_heads(query), split_heads(key_part), split_heads(value_part), split_heads(upstream)))
    return join_heads(grad_query), join_heads(grad_key), join_heads(grad_value)


def reference(queries, key_states, value_states, grad_payload, grad_scale, inputs, lengths):
    usable = (jnp.arange(SEQ_LEN)[None, :] < lengths[:, None]).astype(jnp.float32)
    scaled = grad_payload.astype(jnp.float32).reshape(BATCH, SEQ_LEN, HEADS, HEAD_DIM) * grad_scale.astype(jnp.float32)[..., None]
    upstream = (scaled * usable[:, :, None, None]).reshape(BATCH, SEQ_LEN, HEADS * HEAD_DIM).astype(jnp.bfloat16)
    grad_queries, grad_keys, grad_values = lax.map(clip_backward, (queries, key_states, value_states, upstream, lengths))

    def accumulate(total, items):
        rows, grad_query, grad_key, grad_value = items
        terms = jnp.stack([
            jnp.dot(rows.T, grad_query, preferred_element_type=jnp.float32),
            jnp.dot(rows.T, grad_key, preferred_element_type=jnp.float32),
            jnp.dot(rows.T, grad_value, preferred_element_type=jnp.float32),
        ])
        return total + terms, None

    weight_grad, _ = lax.scan(accumulate, jnp.zeros((3, D, HEADS * HEAD_DIM), jnp.float32), (inputs, grad_queries, grad_keys, grad_values))
    return grad_queries, grad_keys, grad_values, weight_grad
```

```python
import jax
import jax.numpy as jnp
from jax import lax
from jax.experimental import pallas as pl
from jax.experimental.pallas import tpu as pltpu
from jax.sharding import PartitionSpec as P

HEAD_DIM = 64
LANES = 128
ROWS = 512
KEYS = 256
f32 = jnp.float32
bf16 = jnp.bfloat16


def dot(a, b, over=((1,), (0,))):
    return lax.dot_general(a, b, (over, ((), ())), preferred_element_type=f32)


def attention_kernel(
    length_ref, q_ref, k_ref, v_ref, u_ref, dq_ref, dk_ref, dv_ref,
    keys, keys_t, scores, weights, grads, key_total, value_total,
):
    positions = q_ref.shape[0]
    chunks = [slice(at, at + KEYS) for at in range(0, positions, KEYS)]
    length = length_ref[0]
    position = lax.broadcasted_iota(jnp.int32, (positions, LANES), 0)
    lane = lax.broadcasted_iota(jnp.int32, (positions, LANES), 1)
    keys[:, :LANES] = k_ref[...]
    keys[:, LANES:] = jnp.where((lane == 0) & (position >= length), -1e30, 0.0).astype(bf16)
    keys_t[...] = k_ref[...].T
    key_total[...] = jnp.zeros_like(key_total)
    value_total[...] = jnp.zeros_like(value_total)
    lane_row = lax.broadcasted_iota(jnp.int32, (ROWS, LANES), 1)
    ones = jnp.where(lane_row == 0, 1.0, 0.0).astype(bf16)

    def block(index, _):
        start = pl.multiple_of(index * ROWS, ROWS)
        query = q_ref[pl.ds(start, ROWS), :].astype(f32) * HEAD_DIM**-0.5
        upstream = u_ref[pl.ds(start, ROWS), :].astype(f32)
        parts = []
        for head in range(LANES // HEAD_DIM):
            mine = lane_row // HEAD_DIM == head
            q = jnp.where(mine, query, 0.0).astype(bf16)
            u = jnp.where(mine, upstream, 0.0).astype(bf16)
            q_ones = jnp.concatenate([q, ones], axis=1)
            top = jnp.full((8, ROWS), -3e38, f32)
            for chunk in chunks:
                s = dot(keys[chunk, :], q_ones, ((1,), (1,)))
                scores[chunk, :] = s
                top = jnp.maximum(top, jnp.max(s.reshape(KEYS // 8, 8, ROWS), axis=0))
            top = jnp.max(top, axis=0, keepdims=True)
            mass = jnp.zeros((8, ROWS), f32)
            balance = jnp.zeros((8, ROWS), f32)
            for chunk in chunks:
                e = jnp.exp(scores[chunk, :] - top)
                weights[chunk, :] = e
                g = dot(v_ref[chunk, :], u, ((1,), (1,)))
                grads[chunk, :] = g
                mass += jnp.sum(e.reshape(KEYS // 8, 8, ROWS), axis=0)
                balance += jnp.sum((e * g).reshape(KEYS // 8, 8, ROWS), axis=0)
            scale = 1.0 / jnp.sum(mass, axis=0, keepdims=True)
            balance = jnp.sum(balance, axis=0, keepdims=True) * scale
            grad_q = jnp.zeros((HEAD_DIM, ROWS), f32)
            for chunk in chunks:
                p = weights[chunk, :] * scale
                ds = (p * (grads[chunk, :] - balance)).astype(bf16)
                value_total[chunk, :] += dot(p.astype(bf16), u)
                key_total[chunk, :] += dot(ds, q)
                grad_q += dot(keys_t[head * HEAD_DIM : (head + 1) * HEAD_DIM, chunk], ds)
            parts.append(grad_q * HEAD_DIM**-0.5)
        dq_ref[pl.ds(start, ROWS), :] = jnp.concatenate(parts, axis=0).T.astype(bf16)
        return 0

    lax.fori_loop(0, positions // ROWS, block, 0)
    dk_ref[...] = key_total[...].astype(bf16)
    dv_ref[...] = value_total[...].astype(bf16)


def attention_backward(length, q, k, v, u):
    positions = q.shape[0]
    whole = pl.BlockSpec(memory_space=pltpu.VMEM)
    return pl.pallas_call(
        attention_kernel,
        out_shape=[jax.ShapeDtypeStruct(q.shape, bf16)] * 3,
        in_specs=[pl.BlockSpec(memory_space=pltpu.SMEM)] + [whole] * 4,
        out_specs=[whole] * 3,
        scratch_shapes=[
            pltpu.VMEM((positions, 2 * LANES), bf16),
            pltpu.VMEM((LANES, positions), bf16),
            pltpu.VMEM((positions, ROWS), f32),
            pltpu.VMEM((positions, ROWS), f32),
            pltpu.VMEM((positions, ROWS), f32),
            pltpu.VMEM((positions, LANES), f32),
            pltpu.VMEM((positions, LANES), f32),
        ],
        compiler_params=pltpu.CompilerParams(vmem_limit_bytes=48 * 2**20),
        name="attention",
    )(length, q, k, v, u)


def shards(queries, key_states, value_states, grad_payload, grad_scale, inputs, lengths):
    _, positions, width = queries.shape
    _, rows, features = grad_payload.shape
    heads = grad_scale.shape[2]
    owners = features // width
    tokens = lax.axis_index("seq") * rows + jnp.arange(rows)
    live = (tokens < lengths[0]).astype(f32)
    scaled = grad_payload[0].astype(f32).reshape(rows, heads, HEAD_DIM) * grad_scale[0].astype(f32)[..., None]
    upstream = (scaled * live[:, None, None]).astype(bf16).reshape(rows, owners, width)
    upstream = lax.all_to_all(upstream.transpose(1, 0, 2), "seq", split_axis=0, concat_axis=0)
    grads = attention_backward(
        lengths, queries[0], key_states[0], value_states[0], upstream.reshape(positions, width)
    )
    gathered = lax.all_gather(inputs[0], "seq", axis=0, tiled=True)
    terms = jnp.stack([dot(gathered, grad, ((0,), (0,))) for grad in grads])
    weight_grad = lax.psum_scatter(terms, "dp", scatter_dimension=1, tiled=True)
    back = []
    for grad in grads:
        blocks = lax.all_to_all(grad.reshape(owners, rows, width), "seq", split_axis=0, concat_axis=0)
        back.append(blocks.transpose(1, 0, 2).reshape(1, rows, features))
    return (*back, weight_grad)


def solution(mesh):
    return jax.shard_map(
        shards,
        mesh=mesh,
        in_specs=(
            P("dp", None, "seq"),
            P("dp", None, "seq"),
            P("dp", None, "seq"),
            P("dp", "seq", None),
            P("dp", "seq", None),
            P("dp", "seq", None),
            P("dp"),
        ),
        out_specs=(
            P("dp", "seq", None),
            P("dp", "seq", None),
            P("dp", "seq", None),
            P(None, "dp", "seq"),
        ),
        check_vma=False,
    )
```

```python
import functools

import jax
import jax.numpy as jnp
from jax import lax
from jax.experimental import pallas as pl
from jax.experimental.pallas import tpu as pltpu
from jax.sharding import PartitionSpec as P

HEAD_DIM = 64
LANES = 128
ROWS = 512
KEYS = 256
OWNERS = 16
RING = 8
ACROSS = 4
HOPS = RING - 1
MESH = pl.DeviceIdType.MESH
f32 = jnp.float32
bf16 = jnp.bfloat16


def dot(a, b, over=((1,), (0,))):
    return lax.dot_general(a, b, (over, ((), ())), preferred_element_type=f32)


def kernel(
    length_ref, payload_ref, factor_ref, q_hbm, k_hbm, v_hbm, inputs_hbm,
    back_q, back_k, back_v, weight_ref,
    q_ref, k_ref, v_ref, u_ref, sent_up, keys, keys_t, scores, weights, grads, key_total, value_total,
    natural, turned, gathered, kept, to_sibling, from_sibling, staged, terms,
    load_sem, up_send, up_recv, swap_send, swap_recv, right_send, right_recv, left_send, left_recv,
    back_send, back_recv, turned_send, turned_recv, sibling_send, sibling_recv, term_send, term_recv,
):
    positions = q_ref.shape[0]
    tokens = payload_ref.shape[0]
    half = gathered.shape[2]
    columns = half // ACROSS
    depth = columns // 2
    backs = (back_q, back_k, back_v)

    clip, me = lax.axis_index("dp"), lax.axis_index("seq")
    y_hi, x, core = clip // (2 * ACROSS), clip // 2 % ACROSS, clip % 2
    y_lo, z = me // RING, me % RING
    partner = {"dp": clip, "seq": (1 - y_lo) * RING + z}
    right = {"dp": clip, "seq": y_lo * RING + (z + 1) % RING}
    left = {"dp": clip, "seq": y_lo * RING + (z + RING - 1) % RING}
    sibling = {"dp": clip + 1 - 2 * core, "seq": me}
    is_self = (y_hi == y_lo) & (y_lo == core)
    quad = me // 4

    def remote(src, dst, send, recv, device):
        return pltpu.make_async_remote_copy(
            src_ref=src, dst_ref=dst, send_sem=send, recv_sem=recv, device_id=device, device_id_type=MESH
        )

    def rows_of(owner):
        return pl.ds(pl.multiple_of(owner * tokens, tokens), tokens)

    def columns_of(owner):
        return pl.ds(pl.multiple_of(owner * LANES, LANES), LANES)

    loads = [
        pltpu.make_async_copy(src, dst, load_sem.at[n])
        for n, (src, dst) in enumerate(((q_hbm, q_ref), (k_hbm, k_ref), (v_hbm, v_ref)))
    ]
    own_columns = pl.ds(pl.multiple_of(y_lo * half, LANES), half)
    other_columns = pl.ds(pl.multiple_of((1 - y_lo) * half, LANES), half)
    loads.append(pltpu.make_async_copy(inputs_hbm.at[:, own_columns], gathered.at[me], load_sem.at[3]))
    for load in loads:
        load.start()

    barrier = pltpu.get_barrier_semaphore()

    def greet(d, _):
        pl.semaphore_signal(barrier, inc=1, device_id={"dp": clip, "seq": (me + d) % OWNERS}, device_id_type=MESH)
        return 0

    lax.fori_loop(1, OWNERS, greet, 0)
    pl.semaphore_signal(barrier, inc=1, device_id=sibling, device_id_type=MESH)

    def greet_source(n, _):
        @pl.when(jnp.logical_not(is_self & (n == y_hi * ACROSS + x)))
        def _():
            source = {"dp": n // ACROSS * (2 * ACROSS) + n % ACROSS * 2 + y_lo, "seq": y_hi * RING + z}
            pl.semaphore_signal(barrier, inc=1, device_id=source, device_id_type=MESH)

        return 0

    lax.fori_loop(0, 2 * ACROSS, greet_source, 0)

    heads = factor_ref.shape[1]
    spread = lax.broadcasted_iota(jnp.int32, (heads, heads * HEAD_DIM), 1) // HEAD_DIM
    spread = (spread == lax.broadcasted_iota(jnp.int32, spread.shape, 0)).astype(f32).astype(bf16)
    token = me * tokens + lax.broadcasted_iota(jnp.int32, (tokens, heads * HEAD_DIM), 0)
    live = jnp.where(token < length_ref[0], 1.0, 0.0)
    sent_up[...] = (payload_ref[...].astype(f32) * dot(factor_ref[...], spread) * live).astype(bf16)

    pl.semaphore_wait(barrier, OWNERS + 2 * ACROSS - jnp.where(is_self, 1, 0))

    def up_copy(peer):
        return remote(
            sent_up.at[:, columns_of(peer)], u_ref.at[rows_of(me), :], up_send.at[peer], up_recv.at[me],
            {"dp": clip, "seq": peer},
        )

    def up_order(n):
        return (quad + 4 - n // 4) % 4 * 4 + (me + n) % 4

    def send_up(n, _):
        up_copy(up_order(n)).start()
        return 0

    own_up = pltpu.make_async_copy(sent_up.at[:, columns_of(me)], u_ref.at[rows_of(me), :], load_sem.at[4])
    own_up.start()
    lax.fori_loop(1, OWNERS, send_up, 0)

    swap = remote(inputs_hbm.at[:, other_columns], gathered.at[me], swap_send, swap_recv, partner)
    swap.start()

    def block_of(kind, place):
        return jnp.where(kind == 0, y_lo, 1 - y_lo) * RING + (place + RING) % RING

    def hop(to, block, k):
        send, recv = (right_send, right_recv) if to is right else (left_send, left_recv)
        return remote(gathered.at[block], gathered.at[block], send.at[k], recv.at[k], to)

    def right_block(k):
        return block_of(k % 2, z - k // 2 - 1)

    def left_block(k):
        return block_of(jnp.where(k == HOPS - 1, 1, k % 2), z + k // 2 + 1)

    def ring_step(k):
        hop(right, right_block(k), k).wait_recv()

        @pl.when(k + 2 < HOPS)
        def _():
            hop(right, right_block(k), k + 2).start()

        hop(left, left_block(k), k).wait_recv()

        @pl.when(k + 2 < HOPS - 1)
        def _():
            hop(left, left_block(k), k + 2).start()

        @pl.when(k == HOPS - 2)
        def _():
            hop(left, left_block(k), HOPS - 1).start()

    loads[3].wait()
    hop(right, me, 0).start()
    hop(left, me, 0).start()

    chunks = [slice(at, at + KEYS) for at in range(0, positions, KEYS)]
    length = length_ref[0]
    position = lax.broadcasted_iota(jnp.int32, (positions, LANES), 0)
    lane = lax.broadcasted_iota(jnp.int32, (positions, LANES), 1)
    keys[:, LANES:] = jnp.where((lane == 0) & (position >= length), -1e30, 0.0).astype(bf16)
    key_total[...] = jnp.zeros_like(key_total)
    value_total[...] = jnp.zeros_like(value_total)
    for load in loads[:3]:
        load.wait()
    keys[:, :LANES] = k_ref[...]
    keys_t[...] = k_ref[...].T
    lane_row = lax.broadcasted_iota(jnp.int32, (ROWS, LANES), 1)
    ones = jnp.where(lane_row == 0, 1.0, 0.0).astype(bf16)
    own_up.wait()
    swap.wait_recv()
    swapped = partner["seq"]
    hop(right, swapped, 1).start()
    hop(left, swapped, 1).start()

    def back_copy(kind, peer):
        return remote(
            natural.at[kind, rows_of(peer), :], backs[kind].at[:, columns_of(me)],
            back_send.at[kind, peer], back_recv.at[kind, me], {"dp": clip, "seq": peer},
        )

    def back_own(kind):
        return pltpu.make_async_copy(
            natural.at[kind, rows_of(me), :], backs[kind].at[:, columns_of(me)], back_send.at[kind, me]
        )


    def turned_quarter(index):
        at = pl.ds(pl.multiple_of(index * ROWS, ROWS), ROWS)
        view = turned.at[y_lo, pl.ds(0, LANES), at]
        return remote(view, view, turned_send.at[index], turned_recv.at[index], partner)

    def turned_rest():
        view = turned.at[y_lo, pl.ds(LANES, 2 * LANES), :]
        return remote(view, view, turned_send.at[4], turned_recv.at[4], partner)

    def block(step, _):
        index = (quad + step) % 4

        def await_up(n, _):
            peer = index * 4 + n

            @pl.when(peer != me)
            def _():
                remote(
                    sent_up.at[:, columns_of(peer)], u_ref.at[rows_of(peer), :], up_send.at[peer], up_recv.at[peer],
                    {"dp": clip, "seq": peer},
                ).wait_recv()

            return 0

        lax.fori_loop(0, 4, await_up, 0)
        start = pl.multiple_of(index * ROWS, ROWS)
        query = q_ref[pl.ds(start, ROWS), :].astype(f32) * HEAD_DIM**-0.5
        upstream = u_ref[pl.ds(start, ROWS), :].astype(f32)
        parts = []
        for head in range(LANES // HEAD_DIM):
            mine = lane_row // HEAD_DIM == head
            q = jnp.where(mine, query, 0.0).astype(bf16)
            u = jnp.where(mine, upstream, 0.0).astype(bf16)
            q_ones = jnp.concatenate([q, ones], axis=1)
            top = jnp.full((8, ROWS), -3e38, f32)
            for chunk in chunks:
                s = dot(keys[chunk, :], q_ones, ((1,), (1,)))
                scores[chunk, :] = s
                top = jnp.maximum(top, jnp.max(s.reshape(KEYS // 8, 8, ROWS), axis=0))
            top = jnp.max(top, axis=0, keepdims=True)
            mass = jnp.zeros((8, ROWS), f32)
            balance = jnp.zeros((8, ROWS), f32)
            for chunk in chunks:
                e = jnp.exp(scores[chunk, :] - top)
                weights[chunk, :] = e
                g = dot(v_ref[chunk, :], u, ((1,), (1,)))
                grads[chunk, :] = g
                mass += jnp.sum(e.reshape(KEYS // 8, 8, ROWS), axis=0)
                balance += jnp.sum((e * g).reshape(KEYS // 8, 8, ROWS), axis=0)
            scale = 1.0 / jnp.sum(mass, axis=0, keepdims=True)
            balance = jnp.sum(balance, axis=0, keepdims=True) * scale
            grad_q = jnp.zeros((HEAD_DIM, ROWS), f32)
            for chunk in chunks:
                p = weights[chunk, :] * scale
                ds = (p * (grads[chunk, :] - balance)).astype(bf16)
                value_total[chunk, :] += dot(p.astype(bf16), u)
                key_total[chunk, :] += dot(ds, q)
                grad_q += dot(keys_t[head * HEAD_DIM : (head + 1) * HEAD_DIM, chunk], ds)
            parts.append(grad_q * HEAD_DIM**-0.5)
        grad_q = jnp.concatenate(parts, axis=0)
        turned[y_lo, 0:LANES, pl.ds(start, ROWS)] = grad_q.astype(bf16)
        natural[0, pl.ds(start, ROWS), :] = grad_q.T.astype(bf16)
        turned_quarter(index).start()

        def send_back(n, _):
            peer = index * 4 + (me + n) % 4

            @pl.when(peer != me)
            def _():
                back_copy(0, peer).start()

            @pl.when(peer == me)
            def _():
                back_own(0).start()

            return 0

        lax.fori_loop(0, 4, send_back, 0)
        ring_step(step)
        return 0

    lax.fori_loop(0, positions // ROWS, block, 0)

    for kind, total in ((1, key_total), (2, value_total)):
        low = total[...].astype(bf16)
        natural[kind] = low
        turned[y_lo, kind * LANES : (kind + 1) * LANES, :] = low.T
    turned_rest().start()
    for k in range(positions // ROWS, HOPS):
        ring_step(jnp.int32(k))

    def send_rest(n, _):
        peer = (me + n) % OWNERS
        back_copy(1, peer).start()
        back_copy(2, peer).start()
        return 0

    back_own(1).start()
    back_own(2).start()
    lax.fori_loop(1, OWNERS, send_rest, 0)

    for index in range(4):
        turned_quarter(index).wait_recv()
    turned_rest().wait_recv()

    def sibling_copy(n):
        return remote(to_sibling.at[n], from_sibling.at[n], sibling_send.at[n], sibling_recv.at[n], sibling)

    def place_of(n):
        return (x + 1 + n) % ACROSS

    def multiply(n, _):
        at = pl.ds(pl.multiple_of(place_of(n) * columns, LANES), columns)
        part = gathered[:, :, at].reshape(positions, columns)
        to_sibling[n] = dot(turned[1 - core], part).astype(bf16)
        sibling_copy(n).start()
        kept[n] = dot(turned[core], part)
        return 0

    lax.fori_loop(0, ACROSS, multiply, 0)

    def term_copy(n, c):
        target = {"dp": y_lo * (2 * ACROSS) + place_of(n) * 2 + c, "seq": core * RING + z}
        slot = y_hi * ACROSS + x
        return remote(
            staged.at[n, pl.ds(c * depth, depth), :], terms.at[slot], term_send.at[n, c], term_recv.at[slot], target
        )

    def term_own(c):
        return pltpu.make_async_copy(
            staged.at[ACROSS - 1, pl.ds(c * depth, depth), :], terms.at[y_hi * ACROSS + x], term_recv.at[y_hi * ACROSS + x]
        )

    def reduce(n, _):
        sibling_copy(n).wait_recv()
        staged[n] = (kept[n] + from_sibling[n].astype(f32)).T.astype(bf16)
        for c in range(2):
            own = is_self & (n == ACROSS - 1) & (core == c)

            @pl.when(jnp.logical_not(own))
            def _():
                term_copy(n, c).start()

            @pl.when(own)
            def _():
                term_own(c).start()

        return 0

    lax.fori_loop(0, ACROSS, reduce, 0)

    def await_term(n, _):
        pltpu.make_async_copy(terms.at[n], terms.at[n], term_recv.at[n]).wait()
        return 0

    lax.fori_loop(0, 2 * ACROSS, await_term, 0)
    total = terms[0].astype(f32)
    for n in range(1, 2 * ACROSS):
        total += terms[n].astype(f32)
    for kind in range(3):
        weight_ref[kind] = total[:, kind * LANES : (kind + 1) * LANES]

    def await_back(peer, _):
        @pl.when(peer != me)
        def _():
            for kind in range(3):
                remote(
                    natural.at[kind, rows_of(peer), :], backs[kind].at[:, columns_of(peer)],
                    back_send.at[kind, peer], back_recv.at[kind, peer], {"dp": clip, "seq": peer},
                ).wait()
            up_copy(peer).wait_send()

        return 0

    lax.fori_loop(0, OWNERS, await_back, 0)
    for kind in range(3):
        back_own(kind).wait()
    swap.wait_send()
    for k in range(HOPS):
        hop(right, me, k).wait_send()
        hop(left, me, k).wait_send()
    for index in range(4):
        turned_quarter(index).wait_send()
    turned_rest().wait_send()

    def await_sent(n, _):
        sibling_copy(n).wait_send()
        for c in range(2):
            @pl.when(jnp.logical_not(is_self & (n == ACROSS - 1) & (core == c)))
            def _():
                term_copy(n, c).wait_send()

        return 0

    lax.fori_loop(0, ACROSS, await_sent, 0)


def shards(queries, key_states, value_states, grad_payload, grad_scale, inputs, lengths):
    _, positions, width = queries.shape
    _, rows, features = grad_payload.shape
    model = inputs.shape[2]
    half = model // 2
    columns = half // ACROSS
    dma, vmem = pltpu.SemaphoreType.DMA, pltpu.VMEM
    whole = pl.BlockSpec(memory_space=pltpu.VMEM)
    anywhere = pl.BlockSpec(memory_space=pl.ANY)
    *back, weight_grad = pl.pallas_call(
        kernel,
        out_shape=[jax.ShapeDtypeStruct((rows, features), bf16)] * 3
        + [jax.ShapeDtypeStruct((3, columns // 2, width), f32)],
        in_specs=[pl.BlockSpec(memory_space=pltpu.SMEM), whole, whole] + [anywhere] * 4,
        out_specs=[anywhere] * 3 + [whole],
        scratch_shapes=[vmem((positions, width), bf16)] * 4
        + [
            vmem((rows, features), bf16),
            vmem((positions, 2 * width), bf16),
            vmem((width, positions), bf16),
            vmem((positions, ROWS), f32),
            vmem((positions, ROWS), f32),
            vmem((positions, ROWS), f32),
            vmem((positions, width), f32),
            vmem((positions, width), f32),
            vmem((3, positions, width), bf16),
            vmem((2, 3 * width, positions), bf16),
            vmem((OWNERS, rows, half), bf16),
            vmem((ACROSS, 3 * width, columns), f32),
            vmem((ACROSS, 3 * width, columns), bf16),
            vmem((ACROSS, 3 * width, columns), bf16),
            vmem((ACROSS, columns, 3 * width), bf16),
            vmem((2 * ACROSS, columns // 2, 3 * width), bf16),
            dma((5,)),
            dma((OWNERS,)),
            dma((OWNERS,)),
            dma,
            dma,
            dma((HOPS,)),
            dma((HOPS,)),
            dma((HOPS,)),
            dma((HOPS,)),
            dma((3, OWNERS)),
            dma((3, OWNERS)),
            dma((5,)),
            dma((5,)),
            dma((ACROSS,)),
            dma((ACROSS,)),
            dma((ACROSS, 2)),
            dma((2 * ACROSS,)),
        ],
        compiler_params=pltpu.CompilerParams(
            collective_id=0, has_side_effects=True, vmem_limit_bytes=56 * 2**20
        ),
        name="attention_and_weights",
    )(lengths, grad_payload[0], grad_scale[0], queries[0], key_states[0], value_states[0], inputs[0])
    return (*[grad[None] for grad in back], weight_grad)


def solution(mesh):
    return jax.shard_map(
        shards,
        mesh=mesh,
        in_specs=(
            P("dp", None, "seq"),
            P("dp", None, "seq"),
            P("dp", None, "seq"),
            P("dp", "seq", None),
            P("dp", "seq", None),
            P("dp", "seq", None),
            P("dp"),
        ),
        out_specs=(
            P("dp", "seq", None),
            P("dp", "seq", None),
            P("dp", "seq", None),
            P(None, "dp", "seq"),
        ),
        check_vma=False,
    )
```

```python
import functools

import jax
import jax.numpy as jnp
from jax import lax
from jax.experimental import pallas as pl
from jax.experimental.pallas import tpu as pltpu
from jax.sharding import PartitionSpec as P

HEAD_DIM = 64
LANES = 128
ROWS = 512
KEYS = 256
OWNERS = 16
RING = 8
ACROSS = 4
HOPS = RING - 1
MESH = pl.DeviceIdType.MESH
f32 = jnp.float32
bf16 = jnp.bfloat16


def dot(a, b, over=((1,), (0,))):
    return lax.dot_general(a, b, (over, ((), ())), preferred_element_type=f32)


def kernel(
    length_ref, payload_ref, factor_ref, q_hbm, k_hbm, v_hbm, inputs_hbm,
    back_q, back_k, back_v, weight_ref,
    q_ref, k_ref, v_ref, u_ref, sent_up, keys, keys_t, scores, weights, grads, key_total, value_total,
    natural, turned, gathered, weight_total, to_sibling, from_sibling, staged, from_x, leaving, terms,
    load_sem, up_send, up_recv, swap_send, swap_recv, right_send, right_recv, left_send, left_recv,
    back_send, back_recv, turned_send, turned_recv, sibling_send, sibling_recv, sum_send, sum_recv, term_send, term_recv,
):
    positions = q_ref.shape[0]
    tokens = payload_ref.shape[0]
    half = gathered.shape[2]
    columns = half // ACROSS
    depth = columns // 2
    backs = (back_q, back_k, back_v)

    clip, me = lax.axis_index("dp"), lax.axis_index("seq")
    y_hi, x, core = clip // (2 * ACROSS), clip // 2 % ACROSS, clip % 2
    y_lo, z = me // RING, me % RING
    partner = {"dp": clip, "seq": (1 - y_lo) * RING + z}
    right = {"dp": clip, "seq": y_lo * RING + (z + 1) % RING}
    left = {"dp": clip, "seq": y_lo * RING + (z + RING - 1) % RING}
    sibling = {"dp": clip + 1 - 2 * core, "seq": me}

    def along_x(by):
        return {"dp": clip + 2 * ((x + ACROSS + by) % ACROSS - x), "seq": me}

    is_self = (y_hi == y_lo) & (y_lo == core)
    quad = me // 4

    def remote(src, dst, send, recv, device):
        return pltpu.make_async_remote_copy(
            src_ref=src, dst_ref=dst, send_sem=send, recv_sem=recv, device_id=device, device_id_type=MESH
        )

    def rows_of(owner):
        return pl.ds(pl.multiple_of(owner * tokens, tokens), tokens)

    def columns_of(owner):
        return pl.ds(pl.multiple_of(owner * LANES, LANES), LANES)

    loads = [
        pltpu.make_async_copy(src, dst, load_sem.at[n])
        for n, (src, dst) in enumerate(((q_hbm, q_ref), (k_hbm, k_ref), (v_hbm, v_ref)))
    ]
    own_columns = pl.ds(pl.multiple_of(y_lo * half, LANES), half)
    other_columns = pl.ds(pl.multiple_of((1 - y_lo) * half, LANES), half)
    loads.append(pltpu.make_async_copy(inputs_hbm.at[:, own_columns], gathered.at[me], load_sem.at[3]))
    for load in loads:
        load.start()

    barrier = pltpu.get_barrier_semaphore()

    def greet(d, _):
        pl.semaphore_signal(barrier, inc=1, device_id={"dp": clip, "seq": (me + d) % OWNERS}, device_id_type=MESH)
        return 0

    lax.fori_loop(1, OWNERS, greet, 0)
    pl.semaphore_signal(barrier, inc=1, device_id=sibling, device_id_type=MESH)

    for n in range(ACROSS - 1):
        pl.semaphore_signal(barrier, inc=1, device_id=along_x(-1 - n), device_id_type=MESH)
    for n in range(2):
        @pl.when(jnp.logical_not(is_self & (n == y_hi)))
        def _(n=n):
            source = {"dp": n * (2 * ACROSS) + x * 2 + y_lo, "seq": y_hi * RING + z}
            pl.semaphore_signal(barrier, inc=1, device_id=source, device_id_type=MESH)

    pl.semaphore_wait(barrier, OWNERS + ACROSS + 1 - jnp.where(is_self, 1, 0))

    swap = remote(inputs_hbm.at[:, other_columns], gathered.at[me], swap_send, swap_recv, partner)
    swap.start()

    def block_of(kind, place):
        return jnp.where(kind == 0, y_lo, 1 - y_lo) * RING + (place + RING) % RING

    def hop(to, block, k, src=None):
        send, recv = (right_send, right_recv) if to is right else (left_send, left_recv)
        return remote(gathered.at[block] if src is None else src, gathered.at[block], send.at[k], recv.at[k], to)

    def right_block(k):
        return block_of(k % 2, z - k // 2 - 1)

    def left_block(k):
        return block_of(jnp.where(k == HOPS - 1, 1, k % 2), z + k // 2 + 1)

    def ring_step(k):
        hop(right, right_block(k), k).wait_recv()

        @pl.when(k + 2 < HOPS)
        def _():
            hop(right, right_block(k), k + 2).start()

        hop(left, left_block(k), k).wait_recv()

        @pl.when(k + 2 < HOPS - 1)
        def _():
            hop(left, left_block(k), k + 2).start()

        @pl.when(k == HOPS - 2)
        def _():
            hop(left, left_block(k), HOPS - 1).start()

    own_input = inputs_hbm.at[:, own_columns]
    hop(right, me, 0, own_input).start()
    hop(left, me, 0, own_input).start()

    heads = factor_ref.shape[0]
    spread = lax.broadcasted_iota(jnp.int32, (heads, heads * HEAD_DIM), 1) // HEAD_DIM
    spread = (spread == lax.broadcasted_iota(jnp.int32, spread.shape, 0)).astype(f32).astype(bf16)
    token = me * tokens + lax.broadcasted_iota(jnp.int32, (tokens, heads * HEAD_DIM), 0)
    live = jnp.where(token < length_ref[0], 1.0, 0.0)
    sent_up[...] = (payload_ref[...].astype(f32) * dot(factor_ref[...], spread, ((0,), (0,))) * live).astype(bf16)

    def up_copy(peer):
        return remote(
            sent_up.at[:, columns_of(peer)], u_ref.at[rows_of(me), :], up_send.at[peer], up_recv.at[me],
            {"dp": clip, "seq": peer},
        )

    def up_order(n):
        return (quad + 4 - n // 4) % 4 * 4 + (me + n) % 4

    def send_up(n, _):
        up_copy(up_order(n)).start()
        return 0

    own_up = pltpu.make_async_copy(sent_up.at[:, columns_of(me)], u_ref.at[rows_of(me), :], load_sem.at[4])
    own_up.start()
    lax.fori_loop(1, OWNERS, send_up, 0)

    chunks = [slice(at, at + KEYS) for at in range(0, positions, KEYS)]
    length = length_ref[0]
    position = lax.broadcasted_iota(jnp.int32, (positions, LANES), 0)
    lane = lax.broadcasted_iota(jnp.int32, (positions, LANES), 1)
    keys[:, LANES:] = jnp.where((lane == 0) & (position >= length), -1e30, 0.0).astype(bf16)
    key_total[...] = jnp.zeros_like(key_total)
    value_total[...] = jnp.zeros_like(value_total)
    for load in loads:
        load.wait()
    keys[:, :LANES] = k_ref[...]
    keys_t[...] = k_ref[...].T
    lane_row = lax.broadcasted_iota(jnp.int32, (ROWS, LANES), 1)
    ones = jnp.where(lane_row == 0, 1.0, 0.0).astype(bf16)
    own_up.wait()
    swap.wait_recv()
    swapped = partner["seq"]
    hop(right, swapped, 1).start()
    hop(left, swapped, 1).start()

    def back_copy(kind, peer):
        return remote(
            natural.at[kind, rows_of(peer), :], backs[kind].at[:, columns_of(me)],
            back_send.at[kind, peer], back_recv.at[kind, me], {"dp": clip, "seq": peer},
        )

    def back_own(kind):
        return pltpu.make_async_copy(
            natural.at[kind, rows_of(me), :], backs[kind].at[:, columns_of(me)], back_send.at[kind, me]
        )


    def turned_copy(kind, head):
        view = turned.at[y_lo, pl.ds(kind * LANES + head * HEAD_DIM, HEAD_DIM), :]
        return remote(view, view, turned_send.at[kind, head], turned_recv.at[kind, head], partner)

    def block(unit, _):
        head, step = unit // 4, unit % 4
        index = (quad + step) % 4

        def await_up(n, _):
            peer = index * 4 + n

            @pl.when(peer != me)
            def _():
                remote(
                    sent_up.at[:, columns_of(peer)], u_ref.at[rows_of(peer), :], up_send.at[peer], up_recv.at[peer],
                    {"dp": clip, "seq": peer},
                ).wait_recv()

            return 0

        @pl.when(head == 0)
        def _():
            lax.fori_loop(0, 4, await_up, 0)

        start = pl.multiple_of(index * ROWS, ROWS)
        mine = lane_row // HEAD_DIM == head
        q = jnp.where(mine, q_ref[pl.ds(start, ROWS), :].astype(f32) * HEAD_DIM**-0.5, 0.0).astype(bf16)
        u = jnp.where(mine, u_ref[pl.ds(start, ROWS), :].astype(f32), 0.0).astype(bf16)
        q_ones = jnp.concatenate([q, ones], axis=1)
        top = jnp.full((8, ROWS), -3e38, f32)
        for chunk in chunks:
            s = dot(keys[chunk, :], q_ones, ((1,), (1,)))
            scores[chunk, :] = s
            top = jnp.maximum(top, jnp.max(s.reshape(KEYS // 8, 8, ROWS), axis=0))
        top = jnp.max(top, axis=0, keepdims=True)
        mass = jnp.zeros((8, ROWS), f32)
        balance = jnp.zeros((8, ROWS), f32)
        for chunk in chunks:
            e = jnp.exp(scores[chunk, :] - top)
            weights[chunk, :] = e
            g = dot(v_ref[chunk, :], u, ((1,), (1,)))
            grads[chunk, :] = g
            mass += jnp.sum(e.reshape(KEYS // 8, 8, ROWS), axis=0)
            balance += jnp.sum((e * g).reshape(KEYS // 8, 8, ROWS), axis=0)
        scale = 1.0 / jnp.sum(mass, axis=0, keepdims=True)
        balance = jnp.sum(balance, axis=0, keepdims=True) * scale
        grad_q = jnp.zeros((HEAD_DIM, ROWS), f32)
        head_rows = pl.ds(pl.multiple_of(head * HEAD_DIM, HEAD_DIM), HEAD_DIM)
        for chunk in chunks:
            p = weights[chunk, :] * scale
            ds = (p * (grads[chunk, :] - balance)).astype(bf16)
            value_total[chunk, :] += dot(p.astype(bf16), u)
            key_total[chunk, :] += dot(ds, q)
            grad_q += dot(keys_t[head_rows, chunk], ds)
        turned[y_lo, head_rows, pl.ds(start, ROWS)] = (grad_q * HEAD_DIM**-0.5).astype(bf16)

        @pl.when((unit >= 3) & (unit % 2 == 1))
        def _():
            ring_step((unit - 3) // 2)

        @pl.when(step == 3)
        def _():
            turned_copy(0, head).start()
            for kind, total in ((1, key_total), (2, value_total)):
                flat = total[...].astype(bf16).T
                turned[y_lo, pl.ds(pl.multiple_of(kind * LANES + head * HEAD_DIM, HEAD_DIM), HEAD_DIM), :] = jnp.where(
                    head == 0, flat[:HEAD_DIM].astype(f32), flat[HEAD_DIM:].astype(f32)
                ).astype(bf16)
                turned_copy(kind, head).start()

        return 0

    units = positions // ROWS * (LANES // HEAD_DIM)
    lax.fori_loop(0, units, block, 0)

    natural[1] = key_total[...].astype(bf16)
    natural[2] = value_total[...].astype(bf16)
    natural[0] = turned[y_lo, 0:LANES, :].T

    def send_back(kind):
        def send(n, _):
            back_copy(kind, (me + n) % OWNERS).start()
            return 0

        back_own(kind).start()
        lax.fori_loop(1, OWNERS, send, 0)

    def places(sides):
        return [(z + RING + side) % RING for side in sides]

    def product(side, zs, at):
        own = [y * RING + place for place in zs for y in range(2)]
        left_part = jnp.concatenate([turned[side, :, rows_of(block)] for block in own], axis=1)
        return dot(left_part, jnp.concatenate([gathered[block, :, at] for block in own], axis=0))

    def add(side, zs):
        for at in range(0, half, columns):
            weight_total[side, :, at : at + columns] += product(side, zs, slice(at, at + columns))

    def add_pair(side):
        def body(d, _):
            add(side, places((-d, d)))
            return 0

        return body

    def sibling_copy(n):
        return remote(to_sibling.at[n], from_sibling.at[n], sibling_send.at[n], sibling_recv.at[n], sibling)

    def finished(side, n):
        at = pl.ds(pl.multiple_of((x + 1 + n) % ACROSS * columns, LANES), columns)
        return weight_total[side, :, at] + product(side, places((RING // 2,)), at)

    weight_total[...] = jnp.zeros_like(weight_total)
    ring_step(jnp.int32(HOPS - 4))
    add(y_lo, places((0,)))
    lax.fori_loop(1, 3, add_pair(y_lo), 0)
    ring_step(jnp.int32(HOPS - 3))
    ring_step(jnp.int32(HOPS - 2))
    send_back(0)
    add_pair(y_lo)(3, 0)
    for kind in range(3):
        for head in range(2):
            turned_copy(kind, head).wait_recv()
    add(1 - y_lo, places((0,)))
    lax.fori_loop(1, 4, add_pair(1 - y_lo), 0)
    ring_step(jnp.int32(HOPS - 1))

    def give(n, _):
        to_sibling[n] = finished(1 - core, n).astype(bf16)
        sibling_copy(n).start()
        return 0

    lax.fori_loop(0, ACROSS, give, 0)

    def sum_copy(n):
        return remote(staged.at[n], from_x.at[n], sum_send.at[n], sum_recv.at[n], along_x(1 + n))

    def reduce(n, _):
        part = finished(core, n)
        sibling_copy(n).wait_recv()
        staged[n] = (part + from_sibling[n].astype(f32)).astype(bf16)
        sum_copy(n).start()
        return 0

    last = ACROSS - 1
    lax.fori_loop(0, last, reduce, 0)
    send_back(1)
    send_back(2)
    total = finished(core, last)
    sibling_copy(last).wait_recv()
    total += from_sibling[last].astype(f32)
    for n in range(last):
        sum_copy(n).wait_recv()
        total += from_x[n].astype(f32)
    leaving[...] = total.T.astype(bf16)

    def term_copy(c):
        target = {"dp": y_lo * (2 * ACROSS) + x * 2 + c, "seq": core * RING + z}
        return remote(leaving.at[pl.ds(c * depth, depth), :], terms.at[y_hi], term_send.at[c], term_recv.at[y_hi], target)

    def term_own(c):
        return pltpu.make_async_copy(leaving.at[pl.ds(c * depth, depth), :], terms.at[y_hi], term_recv.at[y_hi])

    for c in range(2):
        @pl.when(jnp.logical_not(is_self & (core == c)))
        def _(c=c):
            term_copy(c).start()

        @pl.when(is_self & (core == c))
        def _(c=c):
            term_own(c).start()

    for n in range(2):
        pltpu.make_async_copy(terms.at[n], terms.at[n], term_recv.at[n]).wait()
    total = terms[0].astype(f32) + terms[1].astype(f32)
    for kind in range(3):
        weight_ref[kind] = total[:, kind * LANES : (kind + 1) * LANES]

    def await_back(peer, _):
        @pl.when(peer != me)
        def _():
            for kind in range(3):
                remote(
                    natural.at[kind, rows_of(peer), :], backs[kind].at[:, columns_of(peer)],
                    back_send.at[kind, peer], back_recv.at[kind, peer], {"dp": clip, "seq": peer},
                ).wait()
            up_copy(peer).wait_send()

        return 0

    lax.fori_loop(0, OWNERS, await_back, 0)
    for kind in range(3):
        back_own(kind).wait()
    swap.wait_send()
    for k in range(HOPS):
        hop(right, me, k).wait_send()
        hop(left, me, k).wait_send()
    for kind in range(3):
        for head in range(2):
            turned_copy(kind, head).wait_send()

    for n in range(ACROSS):
        sibling_copy(n).wait_send()
    for n in range(last):
        sum_copy(n).wait_send()
    for c in range(2):
        @pl.when(jnp.logical_not(is_self & (core == c)))
        def _(c=c):
            term_copy(c).wait_send()


def copy_out(*refs):
    count = len(refs) // 2
    copies = [
        pltpu.make_async_copy(src, dst, refs[-1].at[n])
        for n, (src, dst) in enumerate(zip(refs[:count], refs[count:-1]))
    ]
    for copy in copies:
        copy.start()
    for copy in copies:
        copy.wait()


def shards(queries, key_states, value_states, grad_payload, grad_scale, inputs, lengths):
    _, positions, width = queries.shape
    _, rows, features = grad_payload.shape
    model = inputs.shape[2]
    half = model // 2
    columns = half // ACROSS
    dma, vmem = pltpu.SemaphoreType.DMA, pltpu.VMEM
    whole = pl.BlockSpec(memory_space=pltpu.VMEM)
    anywhere = pl.BlockSpec(memory_space=pl.ANY)
    results = pl.pallas_call(
        kernel,
        out_shape=[jax.ShapeDtypeStruct((rows, features), bf16)] * 3
        + [jax.ShapeDtypeStruct((3, columns // 2, width), f32)],
        in_specs=[pl.BlockSpec(memory_space=pltpu.SMEM), whole, whole] + [anywhere] * 4,
        out_specs=[anywhere] * 3 + [whole],
        scratch_shapes=[vmem((positions, width), bf16)] * 4
        + [
            vmem((rows, features), bf16),
            vmem((positions, 2 * width), bf16),
            vmem((width, positions), bf16),
            vmem((positions, ROWS), f32),
            vmem((positions, ROWS), f32),
            vmem((positions, ROWS), f32),
            vmem((positions, width), f32),
            vmem((positions, width), f32),
            vmem((3, positions, width), bf16),
            vmem((2, 3 * width, positions), bf16),
            vmem((OWNERS, rows, half), bf16),
            vmem((2, 3 * width, half), f32),
            vmem((ACROSS, 3 * width, columns), bf16),
            vmem((ACROSS, 3 * width, columns), bf16),
            vmem((ACROSS - 1, 3 * width, columns), bf16),
            vmem((ACROSS - 1, 3 * width, columns), bf16),
            vmem((columns, 3 * width), bf16),
            vmem((2, columns // 2, 3 * width), bf16),
            dma((5,)),
            dma((OWNERS,)),
            dma((OWNERS,)),
            dma,
            dma,
            dma((HOPS,)),
            dma((HOPS,)),
            dma((HOPS,)),
            dma((HOPS,)),
            dma((3, OWNERS)),
            dma((3, OWNERS)),
            dma((3, 2)),
            dma((3, 2)),
            dma((ACROSS,)),
            dma((ACROSS,)),
            dma((ACROSS - 1,)),
            dma((ACROSS - 1,)),
            dma((2,)),
            dma((2,)),
        ],
        compiler_params=pltpu.CompilerParams(
            collective_id=0, has_side_effects=True, vmem_limit_bytes=56 * 2**20
        ),
        name="attention_and_weights",
    )(lengths, grad_payload[0], grad_scale[0].T, queries[0], key_states[0], value_states[0], inputs[0])
    *back, weight_grad = pl.pallas_call(
        copy_out,
        out_shape=[jax.ShapeDtypeStruct(r.shape, r.dtype) for r in results],
        in_specs=[whole] * 4,
        out_specs=[anywhere] * 4,
        scratch_shapes=[dma((4,))],
        name="results",
    )(*results)
    return (*[grad[None] for grad in back], weight_grad)


def solution(mesh):
    return jax.shard_map(
        shards,
        mesh=mesh,
        in_specs=(
            P("dp", None, "seq"),
            P("dp", None, "seq"),
            P("dp", None, "seq"),
            P("dp", "seq", None),
            P("dp", "seq", None),
            P("dp", "seq", None),
            P("dp"),
        ),
        out_specs=(
            P("dp", "seq", None),
            P("dp", "seq", None),
            P("dp", "seq", None),
            P(None, "dp", "seq"),
        ),
        check_vma=False,
    )
```

```python
import functools

import jax
import jax.numpy as jnp
from jax import lax
from jax.experimental import pallas as pl
from jax.experimental.pallas import tpu as pltpu
from jax.sharding import PartitionSpec as P

HEAD_DIM = 64
LANES = 128
ROWS = 512
KEYS = 256
OWNERS = 16
RING = 8
ACROSS = 4
HOPS = RING - 1
MESH = pl.DeviceIdType.MESH
f32 = jnp.float32
bf16 = jnp.bfloat16


def dot(a, b, over=((1,), (0,))):
    return lax.dot_general(a, b, (over, ((), ())), preferred_element_type=f32)


def kernel(
    length_ref, payload_ref, factor_ref, q_hbm, k_hbm, v_hbm, inputs_hbm,
    back_q, back_k, back_v, weight_ref,
    q_ref, k_ref, v_ref, u_ref, sent_up, keys, keys_t, scores, weights, grads, key_total, value_total,
    natural, turned, gathered, weight_total, to_sibling, from_sibling, staged, from_x, own_total, leaving, terms,
    load_sem, up_send, up_recv, swap_send, swap_recv, right_send, right_recv, left_send, left_recv,
    back_send, back_recv, turned_send, turned_recv, block_send, block_recv, sibling_send, sibling_recv, sum_send, sum_recv, term_send, term_recv,
):
    positions = q_ref.shape[0]
    tokens = payload_ref.shape[0]
    half = gathered.shape[2]
    columns = half // ACROSS
    depth = columns // 2
    backs = (back_q, back_k, back_v)

    clip, me = lax.axis_index("dp"), lax.axis_index("seq")
    y_hi, x, core = clip // (2 * ACROSS), clip // 2 % ACROSS, clip % 2
    y_lo, z = me // RING, me % RING
    partner = {"dp": clip, "seq": (1 - y_lo) * RING + z}
    right = {"dp": clip, "seq": y_lo * RING + (z + 1) % RING}
    left = {"dp": clip, "seq": y_lo * RING + (z + RING - 1) % RING}
    sibling = {"dp": clip + 1 - 2 * core, "seq": me}

    def along_x(by):
        return {"dp": clip + 2 * ((x + ACROSS + by) % ACROSS - x), "seq": me}

    is_self = (y_hi == y_lo) & (y_lo == core)
    quad = me // 4

    def remote(src, dst, send, recv, device):
        return pltpu.make_async_remote_copy(
            src_ref=src, dst_ref=dst, send_sem=send, recv_sem=recv, device_id=device, device_id_type=MESH
        )

    def rows_of(owner):
        return pl.ds(pl.multiple_of(owner * tokens, tokens), tokens)

    def columns_of(owner):
        return pl.ds(pl.multiple_of(owner * LANES, LANES), LANES)

    loads = [
        pltpu.make_async_copy(src, dst, load_sem.at[n])
        for n, (src, dst) in enumerate(((q_hbm, q_ref), (k_hbm, k_ref), (v_hbm, v_ref)))
    ]
    own_columns = pl.ds(pl.multiple_of(y_lo * half, LANES), half)
    other_columns = pl.ds(pl.multiple_of((1 - y_lo) * half, LANES), half)
    loads.append(pltpu.make_async_copy(inputs_hbm.at[:, own_columns], gathered.at[me], load_sem.at[3]))
    for load in loads:
        load.start()

    barrier = pltpu.get_barrier_semaphore()

    def greet(d, _):
        pl.semaphore_signal(barrier, inc=1, device_id={"dp": clip, "seq": (me + d) % OWNERS}, device_id_type=MESH)
        return 0

    lax.fori_loop(1, OWNERS, greet, 0)
    pl.semaphore_signal(barrier, inc=1, device_id=sibling, device_id_type=MESH)

    for n in range(ACROSS - 1):
        pl.semaphore_signal(barrier, inc=1, device_id=along_x(-1 - n), device_id_type=MESH)
    for n in range(2):
        @pl.when(jnp.logical_not(is_self & (n == y_hi)))
        def _(n=n):
            source = {"dp": n * (2 * ACROSS) + x * 2 + y_lo, "seq": y_hi * RING + z}
            pl.semaphore_signal(barrier, inc=1, device_id=source, device_id_type=MESH)

    pl.semaphore_wait(barrier, OWNERS + ACROSS + 1 - jnp.where(is_self, 1, 0))

    swap = remote(inputs_hbm.at[:, other_columns], gathered.at[me], swap_send, swap_recv, partner)
    swap.start()

    def block_of(kind, place):
        return jnp.where(kind == 0, y_lo, 1 - y_lo) * RING + (place + RING) % RING

    def hop(to, block, k, src=None):
        send, recv = (right_send, right_recv) if to is right else (left_send, left_recv)
        return remote(gathered.at[block] if src is None else src, gathered.at[block], send.at[k], recv.at[k], to)

    def right_block(k):
        return block_of(k % 2, z - k // 2 - 1)

    def left_block(k):
        return block_of(jnp.where(k == HOPS - 1, 1, k % 2), z + k // 2 + 1)

    def ring_step(k):
        hop(right, right_block(k), k).wait_recv()

        @pl.when(k + 2 < HOPS)
        def _():
            hop(right, right_block(k), k + 2).start()

        hop(left, left_block(k), k).wait_recv()

        @pl.when(k + 2 < HOPS - 1)
        def _():
            hop(left, left_block(k), k + 2).start()

        @pl.when(k == HOPS - 2)
        def _():
            hop(left, left_block(k), HOPS - 1).start()

    own_input = inputs_hbm.at[:, own_columns]
    hop(right, me, 0, own_input).start()
    hop(left, me, 0, own_input).start()

    heads = factor_ref.shape[0]
    spread = lax.broadcasted_iota(jnp.int32, (heads, heads * HEAD_DIM), 1) // HEAD_DIM
    spread = (spread == lax.broadcasted_iota(jnp.int32, spread.shape, 0)).astype(f32).astype(bf16)
    token = me * tokens + lax.broadcasted_iota(jnp.int32, (tokens, heads * HEAD_DIM), 0)
    live = jnp.where(token < length_ref[0], 1.0, 0.0)
    sent_up[...] = (payload_ref[...].astype(f32) * dot(factor_ref[...], spread, ((0,), (0,))) * live).astype(bf16)

    def up_copy(peer):
        return remote(
            sent_up.at[:, columns_of(peer)], u_ref.at[rows_of(me), :], up_send.at[peer], up_recv.at[me],
            {"dp": clip, "seq": peer},
        )

    def up_order(n):
        return (quad + 4 - n // 4) % 4 * 4 + (me + n) % 4

    def send_up(n, _):
        up_copy(up_order(n)).start()
        return 0

    own_up = pltpu.make_async_copy(sent_up.at[:, columns_of(me)], u_ref.at[rows_of(me), :], load_sem.at[4])
    own_up.start()
    lax.fori_loop(1, OWNERS, send_up, 0)

    chunks = [slice(at, at + KEYS) for at in range(0, positions, KEYS)]
    length = length_ref[0]
    position = lax.broadcasted_iota(jnp.int32, (positions, LANES), 0)
    lane = lax.broadcasted_iota(jnp.int32, (positions, LANES), 1)
    keys[:, LANES:] = jnp.where((lane == 0) & (position >= length), -1e30, 0.0).astype(bf16)
    key_total[...] = jnp.zeros_like(key_total)
    value_total[...] = jnp.zeros_like(value_total)
    for load in loads:
        load.wait()
    keys[:, :LANES] = k_ref[...]
    keys_t[...] = k_ref[...].T
    lane_row = lax.broadcasted_iota(jnp.int32, (ROWS, LANES), 1)
    ones = jnp.where(lane_row == 0, 1.0, 0.0).astype(bf16)
    own_up.wait()
    swap.wait_recv()
    swapped = partner["seq"]
    hop(right, swapped, 1).start()
    hop(left, swapped, 1).start()

    def back_copy(kind, peer):
        return remote(
            natural.at[kind, rows_of(peer), :], backs[kind].at[:, columns_of(me)],
            back_send.at[kind, peer], back_recv.at[kind, me], {"dp": clip, "seq": peer},
        )

    def back_own(kind):
        return pltpu.make_async_copy(
            natural.at[kind, rows_of(me), :], backs[kind].at[:, columns_of(me)], back_send.at[kind, me]
        )


    def turned_block(head, index):
        rows = pl.ds(pl.multiple_of(head * HEAD_DIM, HEAD_DIM), HEAD_DIM)
        view = turned.at[y_lo, rows, pl.ds(pl.multiple_of(index * ROWS, ROWS), ROWS)]
        return remote(view, view, block_send.at[head, index], block_recv.at[head, index], partner)

    def turned_copy(kind, head):
        view = turned.at[y_lo, pl.ds(kind * LANES + head * HEAD_DIM, HEAD_DIM), :]
        return remote(view, view, turned_send.at[kind, head], turned_recv.at[kind, head], partner)

    def block(unit, _):
        head, step = unit // 4, unit % 4
        index = (quad + step) % 4

        def await_up(n, _):
            peer = index * 4 + n

            @pl.when(peer != me)
            def _():
                remote(
                    sent_up.at[:, columns_of(peer)], u_ref.at[rows_of(peer), :], up_send.at[peer], up_recv.at[peer],
                    {"dp": clip, "seq": peer},
                ).wait_recv()

            return 0

        @pl.when(head == 0)
        def _():
            lax.fori_loop(0, 4, await_up, 0)

        start = pl.multiple_of(index * ROWS, ROWS)
        mine = lane_row // HEAD_DIM == head
        q = jnp.where(mine, q_ref[pl.ds(start, ROWS), :].astype(f32) * HEAD_DIM**-0.5, 0.0).astype(bf16)
        u = jnp.where(mine, u_ref[pl.ds(start, ROWS), :].astype(f32), 0.0).astype(bf16)
        q_ones = jnp.concatenate([q, ones], axis=1)
        top = jnp.full((8, ROWS), -3e38, f32)
        for chunk in chunks:
            s = dot(keys[chunk, :], q_ones, ((1,), (1,)))
            scores[chunk, :] = s
            top = jnp.maximum(top, jnp.max(s.reshape(KEYS // 8, 8, ROWS), axis=0))
        top = jnp.max(top, axis=0, keepdims=True)
        mass = jnp.zeros((8, ROWS), f32)
        balance = jnp.zeros((8, ROWS), f32)
        for chunk in chunks:
            e = jnp.exp(scores[chunk, :] - top)
            weights[chunk, :] = e
            g = dot(v_ref[chunk, :], u, ((1,), (1,)))
            grads[chunk, :] = g
            mass += jnp.sum(e.reshape(KEYS // 8, 8, ROWS), axis=0)
            balance += jnp.sum((e * g).reshape(KEYS // 8, 8, ROWS), axis=0)
        scale = 1.0 / jnp.sum(mass, axis=0, keepdims=True)
        balance = jnp.sum(balance, axis=0, keepdims=True) * scale
        grad_q = jnp.zeros((HEAD_DIM, ROWS), f32)
        head_rows = pl.ds(pl.multiple_of(head * HEAD_DIM, HEAD_DIM), HEAD_DIM)
        for chunk in chunks:
            p = weights[chunk, :] * scale
            ds = (p * (grads[chunk, :] - balance)).astype(bf16)
            value_total[chunk, :] += dot(p.astype(bf16), u)
            key_total[chunk, :] += dot(ds, q)
            grad_q += dot(keys_t[head_rows, chunk], ds)
        turned[y_lo, head_rows, pl.ds(start, ROWS)] = (grad_q * HEAD_DIM**-0.5).astype(bf16)
        turned_block(head, index).start()

        @pl.when((unit >= 2) & (unit % 2 == 0))
        def _():
            ring_step((unit - 2) // 2)

        @pl.when(step == 3)
        def _():
            for kind, total in ((1, key_total), (2, value_total)):
                flat = total[...].astype(bf16).T
                turned[y_lo, pl.ds(pl.multiple_of(kind * LANES + head * HEAD_DIM, HEAD_DIM), HEAD_DIM), :] = jnp.where(
                    head == 0, flat[:HEAD_DIM].astype(f32), flat[HEAD_DIM:].astype(f32)
                ).astype(bf16)
                turned_copy(kind, head).start()

        return 0

    units = positions // ROWS * (LANES // HEAD_DIM)
    lax.fori_loop(0, units, block, 0)
    ring_step(jnp.int32(HOPS - 4))

    natural[1] = key_total[...].astype(bf16)
    natural[2] = value_total[...].astype(bf16)
    natural[0] = turned[y_lo, 0:LANES, :].T

    def send_back(kind):
        def send(n, _):
            back_copy(kind, (me + n) % OWNERS).start()
            return 0

        back_own(kind).start()
        lax.fori_loop(1, OWNERS, send, 0)

    def places(sides):
        return [(z + RING + side) % RING for side in sides]

    def product(side, zs, at):
        own = [y * RING + place for place in zs for y in range(2)]
        left_part = jnp.concatenate([turned[side, :, rows_of(block)] for block in own], axis=1)
        return dot(left_part, jnp.concatenate([gathered[block, :, at] for block in own], axis=0))

    def add(side, zs):
        for at in range(0, half, columns):
            weight_total[side, :, at : at + columns] += product(side, zs, slice(at, at + columns))

    def add_pair(side):
        def body(d, _):
            add(side, places((-d, d)))
            return 0

        return body

    def sibling_copy(n):
        return remote(to_sibling.at[n], from_sibling.at[n], sibling_send.at[n], sibling_recv.at[n], sibling)

    def finished(side, n):
        at = pl.ds(pl.multiple_of((x + 1 + n) % ACROSS * columns, LANES), columns)
        return weight_total[side, :, at] + product(side, places((RING // 2,)), at)

    weight_total[...] = jnp.zeros_like(weight_total)
    add(y_lo, places((0,)))
    lax.fori_loop(1, 3, add_pair(y_lo), 0)
    ring_step(jnp.int32(HOPS - 3))
    ring_step(jnp.int32(HOPS - 2))
    send_back(0)
    add_pair(y_lo)(3, 0)
    for head in range(2):
        for index in range(4):
            turned_block(head, index).wait_recv()
        for kind in range(1, 3):
            turned_copy(kind, head).wait_recv()
    add(1 - y_lo, places((0,)))
    lax.fori_loop(1, 4, add_pair(1 - y_lo), 0)
    ring_step(jnp.int32(HOPS - 1))

    def give(n, _):
        to_sibling[n] = finished(1 - core, n).astype(bf16)
        sibling_copy(n).start()
        return 0

    lax.fori_loop(0, ACROSS, give, 0)

    def sum_copy(kind, n):
        rows = pl.ds(kind * LANES, LANES)
        return remote(
            staged.at[n, rows, :], from_x.at[n, rows, :], sum_send.at[kind, n], sum_recv.at[kind, n], along_x(1 + n)
        )

    def reduce(n, _):
        part = finished(core, n)
        sibling_copy(n).wait_recv()
        staged[n] = (part + from_sibling[n].astype(f32)).astype(bf16)
        return 0

    last = ACROSS - 1
    lax.fori_loop(0, last, reduce, 0)
    for kind in range(3):
        for n in range(last):
            sum_copy(kind, n).start()
    send_back(1)
    send_back(2)
    total = finished(core, last)
    sibling_copy(last).wait_recv()
    own_total[...] = total + from_sibling[last].astype(f32)

    def term_copy(kind, c):
        target = {"dp": y_lo * (2 * ACROSS) + x * 2 + c, "seq": core * RING + z}
        return remote(
            leaving.at[kind, pl.ds(c * depth, depth), :], terms.at[y_hi, kind],
            term_send.at[kind, c], term_recv.at[y_hi, kind], target,
        )

    def term_own(kind, c):
        return pltpu.make_async_copy(
            leaving.at[kind, pl.ds(c * depth, depth), :], terms.at[y_hi, kind], term_recv.at[y_hi, kind]
        )

    for kind in range(3):
        rows = slice(kind * LANES, (kind + 1) * LANES)
        total = own_total[rows, :]
        for n in range(last):
            sum_copy(kind, n).wait_recv()
            total += from_x[n, rows, :].astype(f32)
        leaving[kind] = total.T.astype(bf16)
        for c in range(2):
            @pl.when(jnp.logical_not(is_self & (core == c)))
            def _(kind=kind, c=c):
                term_copy(kind, c).start()

            @pl.when(is_self & (core == c))
            def _(kind=kind, c=c):
                term_own(kind, c).start()

    for kind in range(3):
        for n in range(2):
            pltpu.make_async_copy(terms.at[n, kind], terms.at[n, kind], term_recv.at[n, kind]).wait()
        weight_ref[kind] = terms[0, kind].astype(f32) + terms[1, kind].astype(f32)

    def await_back(peer, _):
        @pl.when(peer != me)
        def _():
            for kind in range(3):
                remote(
                    natural.at[kind, rows_of(peer), :], backs[kind].at[:, columns_of(peer)],
                    back_send.at[kind, peer], back_recv.at[kind, peer], {"dp": clip, "seq": peer},
                ).wait()
            up_copy(peer).wait_send()

        return 0

    lax.fori_loop(0, OWNERS, await_back, 0)
    for kind in range(3):
        back_own(kind).wait()
    swap.wait_send()
    for k in range(HOPS):
        hop(right, me, k).wait_send()
        hop(left, me, k).wait_send()
    for head in range(2):
        for index in range(4):
            turned_block(head, index).wait_send()
        for kind in range(1, 3):
            turned_copy(kind, head).wait_send()

    for n in range(ACROSS):
        sibling_copy(n).wait_send()
    for kind in range(3):
        for n in range(last):
            sum_copy(kind, n).wait_send()
        for c in range(2):
            @pl.when(jnp.logical_not(is_self & (core == c)))
            def _(kind=kind, c=c):
                term_copy(kind, c).wait_send()


def copy_out(*refs):
    count = 4
    sources, targets, held = refs[:count], refs[count : 2 * count], refs[2 * count : 3 * count]
    arrive, leave = refs[3 * count :]
    into = [pltpu.make_async_copy(sources[n], held[n], arrive.at[n]) for n in range(count)]
    out = [pltpu.make_async_copy(held[n], targets[n], leave.at[n]) for n in range(count)]
    for copy in into:
        copy.start()
    for n in range(count):
        into[n].wait()
        out[n].start()
    for copy in out:
        copy.wait()


def shards(queries, key_states, value_states, grad_payload, grad_scale, inputs, lengths):
    _, positions, width = queries.shape
    _, rows, features = grad_payload.shape
    model = inputs.shape[2]
    half = model // 2
    columns = half // ACROSS
    dma, vmem = pltpu.SemaphoreType.DMA, pltpu.VMEM
    whole = pl.BlockSpec(memory_space=pltpu.VMEM)
    anywhere = pl.BlockSpec(memory_space=pl.ANY)
    results = pl.pallas_call(
        kernel,
        out_shape=[jax.ShapeDtypeStruct((rows, features), bf16)] * 3
        + [jax.ShapeDtypeStruct((3, columns // 2, width), f32)],
        in_specs=[pl.BlockSpec(memory_space=pltpu.SMEM), whole, whole] + [anywhere] * 4,
        out_specs=[anywhere] * 3 + [whole],
        scratch_shapes=[vmem((positions, width), bf16)] * 4
        + [
            vmem((rows, features), bf16),
            vmem((positions, 2 * width), bf16),
            vmem((width, positions), bf16),
            vmem((positions, ROWS), f32),
            vmem((positions, ROWS), f32),
            vmem((positions, ROWS), f32),
            vmem((positions, width), f32),
            vmem((positions, width), f32),
            vmem((3, positions, width), bf16),
            vmem((2, 3 * width, positions), bf16),
            vmem((OWNERS, rows, half), bf16),
            vmem((2, 3 * width, half), f32),
            vmem((ACROSS, 3 * width, columns), bf16),
            vmem((ACROSS, 3 * width, columns), bf16),
            vmem((ACROSS - 1, 3 * width, columns), bf16),
            vmem((ACROSS - 1, 3 * width, columns), bf16),
            vmem((3 * width, columns), f32),
            vmem((3, columns, width), bf16),
            vmem((2, 3, columns // 2, width), bf16),
            dma((5,)),
            dma((OWNERS,)),
            dma((OWNERS,)),
            dma,
            dma,
            dma((HOPS,)),
            dma((HOPS,)),
            dma((HOPS,)),
            dma((HOPS,)),
            dma((3, OWNERS)),
            dma((3, OWNERS)),
            dma((3, 2)),
            dma((3, 2)),
            dma((2, 4)),
            dma((2, 4)),
            dma((ACROSS,)),
            dma((ACROSS,)),
            dma((3, ACROSS - 1)),
            dma((3, ACROSS - 1)),
            dma((3, 2)),
            dma((2, 3)),
        ],
        compiler_params=pltpu.CompilerParams(
            collective_id=0, has_side_effects=True, vmem_limit_bytes=56 * 2**20
        ),
        name="attention_and_weights",
    )(lengths, grad_payload[0], grad_scale[0].T, queries[0], key_states[0], value_states[0], inputs[0])
    *back, weight_grad = pl.pallas_call(
        copy_out,
        out_shape=[jax.ShapeDtypeStruct(r.shape, r.dtype) for r in results],
        in_specs=[anywhere] * 4,
        out_specs=[anywhere] * 4,
        scratch_shapes=[vmem(r.shape, r.dtype) for r in results] + [dma((4,)), dma((4,))],
        name="results",
    )(*results)
    return (*[grad[None] for grad in back], weight_grad)


def solution(mesh):
    return jax.shard_map(
        shards,
        mesh=mesh,
        in_specs=(
            P("dp", None, "seq"),
            P("dp", None, "seq"),
            P("dp", None, "seq"),
            P("dp", "seq", None),
            P("dp", "seq", None),
            P("dp", "seq", None),
            P("dp"),
        ),
        out_specs=(
            P("dp", "seq", None),
            P("dp", "seq", None),
            P("dp", "seq", None),
            P(None, "dp", "seq"),
        ),
        check_vma=False,
    )
```

```python
import functools

import jax
import jax.numpy as jnp
from jax import lax
from jax.experimental import pallas as pl
from jax.experimental.pallas import tpu as pltpu
from jax.sharding import PartitionSpec as P

HEAD_DIM = 64
LANES = 128
ROWS = 512
KEYS = 256
OWNERS = 16
RING = 8
ACROSS = 4
HOPS = RING - 1
MESH = pl.DeviceIdType.MESH
f32 = jnp.float32
bf16 = jnp.bfloat16


def dot(a, b, over=((1,), (0,))):
    return lax.dot_general(a, b, (over, ((), ())), preferred_element_type=f32)


def kernel(
    length_ref, payload_ref, factor_ref, q_hbm, k_hbm, v_hbm, inputs_hbm,
    back_q, back_k, back_v, weight_ref,
    q_ref, k_ref, v_ref, u_ref, sent_up, keys, keys_t, scores, weights, grads, key_total, value_total,
    natural, turned, gathered, weight_total, to_sibling, from_sibling, staged, from_x, own_total, leaving, terms,
    load_sem, up_send, up_recv, swap_send, swap_recv, right_send, right_recv, left_send, left_recv,
    back_send, back_recv, turned_send, turned_recv, block_send, block_recv, sibling_send, sibling_recv, sum_send, sum_recv, term_send, term_recv,
):
    positions = q_ref.shape[0]
    tokens = payload_ref.shape[0]
    half = gathered.shape[2]
    columns = half // ACROSS
    depth = columns // 2
    backs = (back_q, back_k, back_v)

    clip, me = lax.axis_index("dp"), lax.axis_index("seq")
    y_hi, x, core = clip // (2 * ACROSS), clip // 2 % ACROSS, clip % 2
    y_lo, z = me // RING, me % RING
    partner = {"dp": clip, "seq": (1 - y_lo) * RING + z}
    right = {"dp": clip, "seq": y_lo * RING + (z + 1) % RING}
    left = {"dp": clip, "seq": y_lo * RING + (z + RING - 1) % RING}
    sibling = {"dp": clip + 1 - 2 * core, "seq": me}

    def along_x(by):
        return {"dp": clip + 2 * ((x + ACROSS + by) % ACROSS - x), "seq": me}

    is_self = (y_hi == y_lo) & (y_lo == core)
    quad = me // 4

    def remote(src, dst, send, recv, device):
        return pltpu.make_async_remote_copy(
            src_ref=src, dst_ref=dst, send_sem=send, recv_sem=recv, device_id=device, device_id_type=MESH
        )

    def rows_of(owner):
        return pl.ds(pl.multiple_of(owner * tokens, tokens), tokens)

    def columns_of(owner):
        return pl.ds(pl.multiple_of(owner * LANES, LANES), LANES)

    loads = [
        pltpu.make_async_copy(src, dst, load_sem.at[n])
        for n, (src, dst) in enumerate(((q_hbm, q_ref), (k_hbm, k_ref), (v_hbm, v_ref)))
    ]
    own_columns = pl.ds(pl.multiple_of(y_lo * half, LANES), half)
    other_columns = pl.ds(pl.multiple_of((1 - y_lo) * half, LANES), half)
    loads.append(pltpu.make_async_copy(inputs_hbm.at[:, own_columns], gathered.at[me], load_sem.at[3]))
    barrier = pltpu.get_barrier_semaphore()

    def greet(d, _):
        pl.semaphore_signal(barrier, inc=1, device_id={"dp": clip, "seq": (me + d) % OWNERS}, device_id_type=MESH)
        return 0

    lax.fori_loop(1, OWNERS, greet, 0)
    pl.semaphore_signal(barrier, inc=1, device_id=sibling, device_id_type=MESH)

    for n in range(ACROSS - 1):
        pl.semaphore_signal(barrier, inc=1, device_id=along_x(-1 - n), device_id_type=MESH)
    for n in range(2):
        @pl.when(jnp.logical_not(is_self & (n == y_hi)))
        def _(n=n):
            source = {"dp": n * (2 * ACROSS) + x * 2 + y_lo, "seq": y_hi * RING + z}
            pl.semaphore_signal(barrier, inc=1, device_id=source, device_id_type=MESH)

    for load in loads:
        load.start()

    heads = factor_ref.shape[0]
    spread = lax.broadcasted_iota(jnp.int32, (heads, heads * HEAD_DIM), 1) // HEAD_DIM
    spread = (spread == lax.broadcasted_iota(jnp.int32, spread.shape, 0)).astype(f32).astype(bf16)
    token = me * tokens + lax.broadcasted_iota(jnp.int32, (tokens, heads * HEAD_DIM), 0)
    live = jnp.where(token < length_ref[0], 1.0, 0.0)
    sent_up[...] = (payload_ref[...].astype(f32) * dot(factor_ref[...], spread, ((0,), (0,))) * live).astype(bf16)

    pl.semaphore_wait(barrier, OWNERS + ACROSS + 1 - jnp.where(is_self, 1, 0))

    swap = remote(inputs_hbm.at[:, other_columns], gathered.at[me], swap_send, swap_recv, partner)
    swap.start()

    def block_of(kind, place):
        return jnp.where(kind == 0, y_lo, 1 - y_lo) * RING + (place + RING) % RING

    def hop(to, block, k, src=None):
        send, recv = (right_send, right_recv) if to is right else (left_send, left_recv)
        return remote(gathered.at[block] if src is None else src, gathered.at[block], send.at[k], recv.at[k], to)

    def right_block(k):
        return block_of(k % 2, z - k // 2 - 1)

    def left_block(k):
        return block_of(jnp.where(k == HOPS - 1, 1, k % 2), z + k // 2 + 1)

    def ring_step(k):
        hop(right, right_block(k), k).wait_recv()

        @pl.when(k + 2 < HOPS)
        def _():
            hop(right, right_block(k), k + 2).start()

        hop(left, left_block(k), k).wait_recv()

        @pl.when(k + 2 < HOPS - 1)
        def _():
            hop(left, left_block(k), k + 2).start()

        @pl.when(k == HOPS - 2)
        def _():
            hop(left, left_block(k), HOPS - 1).start()

    own_input = inputs_hbm.at[:, own_columns]
    hop(right, me, 0, own_input).start()
    hop(left, me, 0, own_input).start()

    def up_copy(peer):
        return remote(
            sent_up.at[:, columns_of(peer)], u_ref.at[rows_of(me), :], up_send.at[peer], up_recv.at[me],
            {"dp": clip, "seq": peer},
        )

    def up_order(n):
        return (quad + 4 - n // 4) % 4 * 4 + (me + n) % 4

    def send_up(n, _):
        up_copy(up_order(n)).start()
        return 0

    own_up = pltpu.make_async_copy(sent_up.at[:, columns_of(me)], u_ref.at[rows_of(me), :], load_sem.at[4])
    own_up.start()
    lax.fori_loop(1, OWNERS, send_up, 0)

    chunks = [slice(at, at + KEYS) for at in range(0, positions, KEYS)]
    length = length_ref[0]
    position = lax.broadcasted_iota(jnp.int32, (positions, LANES), 0)
    lane = lax.broadcasted_iota(jnp.int32, (positions, LANES), 1)
    keys[:, LANES:] = jnp.where((lane == 0) & (position >= length), -1e30, 0.0).astype(bf16)
    weight_total[...] = jnp.zeros_like(weight_total)
    key_total[...] = jnp.zeros_like(key_total)
    value_total[...] = jnp.zeros_like(value_total)
    for load in loads:
        load.wait()
    keys[:, :LANES] = k_ref[...]
    keys_t[...] = k_ref[...].T
    lane_row = lax.broadcasted_iota(jnp.int32, (ROWS, LANES), 1)
    ones = jnp.where(lane_row == 0, 1.0, 0.0).astype(bf16)
    own_up.wait()
    swap.wait_recv()
    swapped = partner["seq"]
    hop(right, swapped, 1).start()
    hop(left, swapped, 1).start()

    def back_copy(kind, peer):
        return remote(
            natural.at[kind, rows_of(peer), :], backs[kind].at[:, columns_of(me)],
            back_send.at[kind, peer], back_recv.at[kind, me], {"dp": clip, "seq": peer},
        )

    def back_own(kind):
        return pltpu.make_async_copy(
            natural.at[kind, rows_of(me), :], backs[kind].at[:, columns_of(me)], back_send.at[kind, me]
        )


    def turned_block(head, index):
        rows = pl.ds(pl.multiple_of(head * HEAD_DIM, HEAD_DIM), HEAD_DIM)
        view = turned.at[y_lo, rows, pl.ds(pl.multiple_of(index * ROWS, ROWS), ROWS)]
        return remote(view, view, block_send.at[head, index], block_recv.at[head, index], partner)

    def turned_copy(kind, head):
        view = turned.at[y_lo, pl.ds(kind * LANES + head * HEAD_DIM, HEAD_DIM), :]
        return remote(view, view, turned_send.at[kind, head], turned_recv.at[kind, head], partner)

    def block(unit, _):
        head, step = unit // 4, unit % 4
        index = (quad + step) % 4

        def await_up(n, _):
            peer = index * 4 + n

            @pl.when(peer != me)
            def _():
                remote(
                    sent_up.at[:, columns_of(peer)], u_ref.at[rows_of(peer), :], up_send.at[peer], up_recv.at[peer],
                    {"dp": clip, "seq": peer},
                ).wait_recv()

            return 0

        @pl.when(head == 0)
        def _():
            lax.fori_loop(0, 4, await_up, 0)

        start = pl.multiple_of(index * ROWS, ROWS)
        mine = lane_row // HEAD_DIM == head
        q = jnp.where(mine, q_ref[pl.ds(start, ROWS), :].astype(f32) * HEAD_DIM**-0.5, 0.0).astype(bf16)
        u = jnp.where(mine, u_ref[pl.ds(start, ROWS), :].astype(f32), 0.0).astype(bf16)
        q_ones = jnp.concatenate([q, ones], axis=1)
        top = jnp.full((8, ROWS), -3e38, f32)
        for chunk in chunks:
            s = dot(keys[chunk, :], q_ones, ((1,), (1,)))
            scores[chunk, :] = s
            top = jnp.maximum(top, jnp.max(s.reshape(KEYS // 8, 8, ROWS), axis=0))
        top = jnp.max(top, axis=0, keepdims=True)
        mass = jnp.zeros((8, ROWS), f32)
        balance = jnp.zeros((8, ROWS), f32)
        for chunk in chunks:
            e = jnp.exp(scores[chunk, :] - top)
            weights[chunk, :] = e
            g = dot(v_ref[chunk, :], u, ((1,), (1,)))
            grads[chunk, :] = g
            mass += jnp.sum(e.reshape(KEYS // 8, 8, ROWS), axis=0)
            balance += jnp.sum((e * g).reshape(KEYS // 8, 8, ROWS), axis=0)
        scale = 1.0 / jnp.sum(mass, axis=0, keepdims=True)
        balance = jnp.sum(balance, axis=0, keepdims=True) * scale
        grad_q = jnp.zeros((HEAD_DIM, ROWS), f32)
        head_rows = pl.ds(pl.multiple_of(head * HEAD_DIM, HEAD_DIM), HEAD_DIM)
        for chunk in chunks:
            p = weights[chunk, :] * scale
            ds = (p * (grads[chunk, :] - balance)).astype(bf16)
            value_total[chunk, :] += dot(p.astype(bf16), u)
            key_total[chunk, :] += dot(ds, q)
            grad_q += dot(keys_t[head_rows, chunk], ds)
        turned[y_lo, head_rows, pl.ds(start, ROWS)] = (grad_q * HEAD_DIM**-0.5).astype(bf16)
        turned_block(head, index).start()

        @pl.when((unit >= 2) & (unit % 2 == 0))
        def _():
            ring_step((unit - 2) // 2)

        @pl.when(step == 3)
        def _():
            for kind, total in ((1, key_total), (2, value_total)):
                flat = total[...].astype(bf16).T
                turned[y_lo, pl.ds(pl.multiple_of(kind * LANES + head * HEAD_DIM, HEAD_DIM), HEAD_DIM), :] = jnp.where(
                    head == 0, flat[:HEAD_DIM].astype(f32), flat[HEAD_DIM:].astype(f32)
                ).astype(bf16)
                turned_copy(kind, head).start()

        return 0

    units = positions // ROWS * (LANES // HEAD_DIM)
    lax.fori_loop(0, units, block, 0)
    ring_step(jnp.int32(HOPS - 4))

    natural[1] = key_total[...].astype(bf16)
    natural[2] = value_total[...].astype(bf16)
    natural[0] = turned[y_lo, 0:LANES, :].T

    def send_back(kind):
        def send(n, _):
            back_copy(kind, (me + n) % OWNERS).start()
            return 0

        back_own(kind).start()
        lax.fori_loop(1, OWNERS, send, 0)

    def places(sides):
        return [(z + RING + side) % RING for side in sides]

    def product(side, zs, at):
        own = [y * RING + place for place in zs for y in range(2)]
        left_part = jnp.concatenate([turned[side, :, rows_of(block)] for block in own], axis=1)
        return dot(left_part, jnp.concatenate([gathered[block, :, at] for block in own], axis=0))

    def add(side, zs):
        for at in range(0, half, columns):
            weight_total[side, :, at : at + columns] += product(side, zs, slice(at, at + columns))

    def add_pair(side):
        def body(d, _):
            add(side, places((-d, d)))
            return 0

        return body

    def sibling_copy(n):
        return remote(to_sibling.at[n], from_sibling.at[n], sibling_send.at[n], sibling_recv.at[n], sibling)

    def finished(side, n):
        at = pl.ds(pl.multiple_of((x + 1 + n) % ACROSS * columns, LANES), columns)
        return weight_total[side, :, at] + product(side, places((RING // 2,)), at)

    add(y_lo, places((0,)))
    lax.fori_loop(1, 3, add_pair(y_lo), 0)
    ring_step(jnp.int32(HOPS - 3))
    ring_step(jnp.int32(HOPS - 2))
    send_back(0)
    add_pair(y_lo)(3, 0)
    for head in range(2):
        for index in range(4):
            turned_block(head, index).wait_recv()
        for kind in range(1, 3):
            turned_copy(kind, head).wait_recv()
    add(1 - y_lo, places((0,)))
    lax.fori_loop(1, 4, add_pair(1 - y_lo), 0)
    ring_step(jnp.int32(HOPS - 1))

    def give(n, _):
        to_sibling[n] = finished(1 - core, n).astype(bf16)
        sibling_copy(n).start()
        return 0

    lax.fori_loop(0, ACROSS, give, 0)

    def sum_copy(kind, n):
        rows = pl.ds(kind * LANES, LANES)
        return remote(
            staged.at[n, rows, :], from_x.at[n, rows, :], sum_send.at[kind, n], sum_recv.at[kind, n], along_x(1 + n)
        )

    def reduce(n, _):
        part = finished(core, n)
        sibling_copy(n).wait_recv()
        staged[n] = (part + from_sibling[n].astype(f32)).astype(bf16)
        return 0

    last = ACROSS - 1
    lax.fori_loop(0, last, reduce, 0)
    for kind in range(3):
        for n in range(last):
            sum_copy(kind, n).start()
    send_back(1)
    send_back(2)
    total = finished(core, last)
    sibling_copy(last).wait_recv()
    own_total[...] = total + from_sibling[last].astype(f32)

    def term_copy(kind, c):
        target = {"dp": y_lo * (2 * ACROSS) + x * 2 + c, "seq": core * RING + z}
        return remote(
            leaving.at[kind, pl.ds(c * depth, depth), :], terms.at[y_hi, kind],
            term_send.at[kind, c], term_recv.at[y_hi, kind], target,
        )

    def term_own(kind, c):
        return pltpu.make_async_copy(
            leaving.at[kind, pl.ds(c * depth, depth), :], terms.at[y_hi, kind], term_recv.at[y_hi, kind]
        )

    for kind in range(3):
        rows = slice(kind * LANES, (kind + 1) * LANES)
        total = own_total[rows, :]
        for n in range(last):
            sum_copy(kind, n).wait_recv()
            total += from_x[n, rows, :].astype(f32)
        leaving[kind] = total.T.astype(bf16)
        for c in range(2):
            @pl.when(jnp.logical_not(is_self & (core == c)))
            def _(kind=kind, c=c):
                term_copy(kind, c).start()

            @pl.when(is_self & (core == c))
            def _(kind=kind, c=c):
                term_own(kind, c).start()

    for kind in range(3):
        for n in range(2):
            pltpu.make_async_copy(terms.at[n, kind], terms.at[n, kind], term_recv.at[n, kind]).wait()
        weight_ref[kind] = terms[0, kind].astype(f32) + terms[1, kind].astype(f32)

    def await_back(peer, _):
        @pl.when(peer != me)
        def _():
            for kind in range(3):
                remote(
                    natural.at[kind, rows_of(peer), :], backs[kind].at[:, columns_of(peer)],
                    back_send.at[kind, peer], back_recv.at[kind, peer], {"dp": clip, "seq": peer},
                ).wait()
            up_copy(peer).wait_send()

        return 0

    lax.fori_loop(0, OWNERS, await_back, 0)
    for kind in range(3):
        back_own(kind).wait()
    swap.wait_send()
    for k in range(HOPS):
        hop(right, me, k).wait_send()
        hop(left, me, k).wait_send()
    for head in range(2):
        for index in range(4):
            turned_block(head, index).wait_send()
        for kind in range(1, 3):
            turned_copy(kind, head).wait_send()

    for n in range(ACROSS):
        sibling_copy(n).wait_send()
    for kind in range(3):
        for n in range(last):
            sum_copy(kind, n).wait_send()
        for c in range(2):
            @pl.when(jnp.logical_not(is_self & (core == c)))
            def _(kind=kind, c=c):
                term_copy(kind, c).wait_send()


def copy_out(*refs):
    count = 4
    sources, targets, held = refs[:count], refs[count : 2 * count], refs[2 * count : 3 * count]
    arrive, leave = refs[3 * count :]
    into = [pltpu.make_async_copy(sources[n], held[n], arrive.at[n]) for n in range(count)]
    out = [pltpu.make_async_copy(held[n], targets[n], leave.at[n]) for n in range(count)]
    for copy in into:
        copy.start()
    for n in range(count):
        into[n].wait()
        out[n].start()
    for copy in out:
        copy.wait()


def shards(queries, key_states, value_states, grad_payload, grad_scale, inputs, lengths):
    _, positions, width = queries.shape
    _, rows, features = grad_payload.shape
    model = inputs.shape[2]
    half = model // 2
    columns = half // ACROSS
    dma, vmem = pltpu.SemaphoreType.DMA, pltpu.VMEM
    whole = pl.BlockSpec(memory_space=pltpu.VMEM)
    anywhere = pl.BlockSpec(memory_space=pl.ANY)
    results = pl.pallas_call(
        kernel,
        out_shape=[jax.ShapeDtypeStruct((rows, features), bf16)] * 3
        + [jax.ShapeDtypeStruct((3, columns // 2, width), f32)],
        in_specs=[pl.BlockSpec(memory_space=pltpu.SMEM), whole, whole] + [anywhere] * 4,
        out_specs=[anywhere] * 3 + [whole],
        scratch_shapes=[vmem((positions, width), bf16)] * 4
        + [
            vmem((rows, features), bf16),
            vmem((positions, 2 * width), bf16),
            vmem((width, positions), bf16),
            vmem((positions, ROWS), f32),
            vmem((positions, ROWS), f32),
            vmem((positions, ROWS), f32),
            vmem((positions, width), f32),
            vmem((positions, width), f32),
            vmem((3, positions, width), bf16),
            vmem((2, 3 * width, positions), bf16),
            vmem((OWNERS, rows, half), bf16),
            vmem((2, 3 * width, half), f32),
            vmem((ACROSS, 3 * width, columns), bf16),
            vmem((ACROSS, 3 * width, columns), bf16),
            vmem((ACROSS - 1, 3 * width, columns), bf16),
            vmem((ACROSS - 1, 3 * width, columns), bf16),
            vmem((3 * width, columns), f32),
            vmem((3, columns, width), bf16),
            vmem((2, 3, columns // 2, width), bf16),
            dma((5,)),
            dma((OWNERS,)),
            dma((OWNERS,)),
            dma,
            dma,
            dma((HOPS,)),
            dma((HOPS,)),
            dma((HOPS,)),
            dma((HOPS,)),
            dma((3, OWNERS)),
            dma((3, OWNERS)),
            dma((3, 2)),
            dma((3, 2)),
            dma((2, 4)),
            dma((2, 4)),
            dma((ACROSS,)),
            dma((ACROSS,)),
            dma((3, ACROSS - 1)),
            dma((3, ACROSS - 1)),
            dma((3, 2)),
            dma((2, 3)),
        ],
        compiler_params=pltpu.CompilerParams(
            collective_id=0, has_side_effects=True, vmem_limit_bytes=56 * 2**20
        ),
        name="attention_and_weights",
    )(lengths, grad_payload[0], grad_scale[0].T, queries[0], key_states[0], value_states[0], inputs[0])
    *back, weight_grad = pl.pallas_call(
        copy_out,
        out_shape=[jax.ShapeDtypeStruct(r.shape, r.dtype) for r in results],
        in_specs=[anywhere] * 4,
        out_specs=[anywhere] * 4,
        scratch_shapes=[vmem(r.shape, r.dtype) for r in results] + [dma((4,)), dma((4,))],
        name="results",
    )(*results)
    return (*[grad[None] for grad in back], weight_grad)


def solution(mesh):
    return jax.shard_map(
        shards,
        mesh=mesh,
        in_specs=(
            P("dp", None, "seq"),
            P("dp", None, "seq"),
            P("dp", None, "seq"),
            P("dp", "seq", None),
            P("dp", "seq", None),
            P("dp", "seq", None),
            P("dp"),
        ),
        out_specs=(
            P("dp", "seq", None),
            P("dp", "seq", None),
            P("dp", "seq", None),
            P(None, "dp", "seq"),
        ),
        check_vma=False,
    )
```
